128 devices in a mesh: layer: 4 (over y_lo, core), shard: 32 (over x, z, y_hi).
Axes of the slice: x: 4, y: 4 (y_hi: 2, y_lo: 2; y = y_hi * 2 + y_lo), z: 4, core: 2. Of those that a mesh axis runs over, the one named last changes fastest.
Arguments:
- layer_inputs: bfloat16 [4, 1536, 5120], P('layer', 'shard'), may hold values from -6 to 6
- output_grads: bfloat16 [4, 1536, 16384], P('layer', 'shard'), may hold values from -6 to 6
- input_basis: bfloat16 [4, 10, 512, 512], P('layer'), may hold values from -0.25 to 0.25
- grad_basis: bfloat16 [4, 32, 512, 512], P('layer', 'shard'), may hold values from -0.25 to 0.25
- eigenvalues: float32 [4, 16384, 5120], P('layer', 'shard'), may hold values from 0.1 to 10
- layer_table: int32 [4], replicated, may hold values from 0 to 3, each once
- batch_ids: int32 [16], replicated, may hold values from 0 to 3
Outputs:
- scores: float32 [16, 16], replicated
- batch_scores: float32 [16, 4], replicated
- layer_totals: float32 [4, 16], replicated
The draws below stay inside these ranges and needn't reach their ends.
All inputs are finite; a program needn't handle non-finite values.
Results may differ from the reference program's by a relative error of at most 0.0063.
Values may be sent and summed in bfloat16 or wider, within the bound.
A program may use at most 384 MiB of HBM per device.

```python
import math
import jax
import jax.numpy as jnp
from jax import lax

D = 5120
BLK = 512
NQ = 16
SQ = 32
NT = 16
ST = 64
NB = 4
FFW = 16384
LAYERS = 4
QTOK = 512
TTOK = 1024


def place_ends(array, key, least, high):
    longest = array.shape.index(max(array.shape))
    spots = []
    for shift in (0, 1):
        where = [jax.random.randint(jax.random.fold_in(key, axis), (), 0, length) for axis, length in enumerate(array.shape)]
        where[longest] = (where[longest] + shift) % array.shape[longest]
        spots.append(tuple(where))
    return array.at[spots[0]].set(least).at[spots[1]].set(high)


def steps_of(stream_key, shape, pieces, least, high):
    loudness = 1.0
    for axis_at, parts in pieces:
        steps = jax.random.uniform(jax.random.fold_in(jax.random.fold_in(stream_key, 6), axis_at), (parts,), jnp.float32, least / len(pieces), high / len(pieces))
        loudness = loudness * jnp.repeat(jnp.exp(steps), shape[axis_at] // parts).reshape((-1,) + (1,) * (len(shape) - 1 - axis_at))
    return loudness


def centred(stream_key, dims, width, reach, split=(), kind=jnp.bfloat16):
    result = width * jax.random.normal(stream_key, dims, jnp.float32)
    if split:
        result = result * steps_of(stream_key, dims, split, -0.22, 0.18)
    return jnp.clip(result, -reach, reach).astype(kind)


def setup_inputs(seed: int = 0) -> dict:
    streams_of = jax.random.split(jax.random.key(seed), 8)
    return {
        "layer_inputs": centred(streams_of[0], (LAYERS, QTOK + TTOK, D), 1.0, 6.0, ((0, 4), (1, 32))),
        "output_grads": centred(streams_of[1], (LAYERS, QTOK + TTOK, FFW), 1.0, 6.0, ((0, 4), (1, 32))),
        "input_basis": centred(streams_of[2], (LAYERS, D // BLK, BLK, BLK), BLK ** -0.5, 0.25, ((0, 4),)),
        "grad_basis": centred(streams_of[3], (LAYERS, FFW // BLK, BLK, BLK), BLK ** -0.5, 0.25, ((0, 4), (1, 32))),
        "eigenvalues": jnp.clip(jnp.exp(math.log(10.0) - 4.6051702 * jax.random.uniform(streams_of[4], (LAYERS, FFW, D), jnp.float32) ** steps_of(streams_of[4], (LAYERS, FFW, D), ((0, 4), (1, 32)), -0.2, 0.2)), 0.1, 10.0),
        "layer_table": jax.random.permutation(streams_of[5], LAYERS).astype(jnp.int32),
        "batch_ids": place_ends(jax.random.randint(streams_of[6], (NT,), 0, NB), jax.random.fold_in(streams_of[6], 1), 0, NB - 1).astype(jnp.int32),
    }


DAMPING = 0.1

def project_inputs(row_block, bases):
    block_count = bases.shape[0]
    block_width = bases.shape[1]
    blocked = row_block.reshape(row_block.shape[0], block_count, block_width).astype(jnp.float32)
    product = jnp.einsum('rkc,kcd->rkd', blocked, bases.astype(jnp.float32))
    return product.reshape(row_block.shape[0], block_count * block_width).astype(jnp.bfloat16)

def reference(layer_inputs, output_grads, input_basis, grad_basis, eigenvalues, layer_table, batch_ids):
    query_rows = NQ * SQ
    norm_factor = 1.0 / math.sqrt(FFW * D * SQ * ST)
    per_layer = []
    for slot in range(LAYERS):
        input_proj = project_inputs(layer_inputs[slot], input_basis[slot])
        query_in = input_proj[:query_rows].reshape(NQ, SQ, D).astype(jnp.float32)
        train_in = input_proj[query_rows:].reshape(NT, ST, D).astype(jnp.float32)
        grads_here = output_grads[slot]
        bases_here = grad_basis[slot]
        values_here = eigenvalues[slot]

        def one_block(block_index):
            start = (block_index * BLK).astype(jnp.int32)
            columns = lax.dynamic_slice_in_dim(grads_here, start, BLK, 1)
            block_basis = lax.dynamic_index_in_dim(bases_here, block_index, 0, keepdims=False)
            grad_proj = jnp.dot(columns, block_basis, preferred_element_type=jnp.float32).astype(jnp.bfloat16)
            inverse = 1.0 / (lax.dynamic_slice_in_dim(values_here, start, BLK, 0) + DAMPING)
            query_out = grad_proj[:query_rows].reshape(NQ, SQ, BLK).astype(jnp.float32)
            train_out = grad_proj[query_rows:].reshape(NT, ST, BLK).astype(jnp.float32)
            query_grad = jnp.einsum('qsi,qsj->qij', query_out, query_in)
            weighted = (query_grad * inverse[None]).astype(jnp.bfloat16)
            train_grad = jnp.einsum('tsi,tsj->tij', train_out, train_in).astype(jnp.bfloat16)
            return jnp.einsum('qij,tij->qt', weighted.astype(jnp.float32), train_grad.astype(jnp.float32))
        partials = lax.map(one_block, jnp.arange(FFW // BLK, dtype=jnp.int32))
        per_layer.append(norm_factor * lax.optimization_barrier(jnp.sum(partials, axis=0)))
    layer_scores = jnp.stack(per_layer)
    scores = lax.optimization_barrier(jnp.sum(layer_scores, axis=0))
    batch_marks = (batch_ids[:, None] == jnp.arange(NB, dtype=jnp.int32)[None, :]).astype(jnp.float32)
    batch_scores = lax.optimization_barrier(jnp.sum(scores[:, :, None] * batch_marks[None, :, :], axis=1))
    layer_marks = (layer_table[:, None] == jnp.arange(LAYERS, dtype=jnp.int32)[None, :]).astype(jnp.float32)
    layer_sums = lax.optimization_barrier(jnp.sum(layer_scores, axis=2))
    layer_totals = lax.optimization_barrier(jnp.sum(layer_marks[:, :, None] * layer_sums[:, None, :], axis=0))
    return (scores, batch_scores, layer_totals)
```

```python
import functools
import math

import jax
import jax.numpy as jnp
from jax import lax
from jax.experimental import pallas as pl
from jax.experimental.pallas import tpu as pltpu
from jax.sharding import PartitionSpec as P

NQ = 16
SQ = 32
NT = 16
ST = 64
NB = 4
DAMPING = 0.1

D = 5120
BLK = 512
CHUNKS = D // BLK
HALF = BLK // 2
SHARDS = 32
LAYERS = 4
ROWS = 48
QTOK = NQ * SQ
GROUP = 4
LEAD = 4
MESH = pl.DeviceIdType.MESH
F32 = jnp.float32
BF = jnp.bfloat16


def where_am_i():
    shard = lax.axis_index("shard")
    return {"x": shard // 8, "z": (shard // 2) % 4, "h": shard % 2}


def shifted(at, axis, step):
    out = dict(at)
    out[axis] = (at[axis] + step + 4) % (2 if axis == "h" else 4)
    return out


def device_of(at):
    return (lax.axis_index("layer"), (at["x"] * 4 + at["z"]) * 2 + at["h"])


def region(buf, c, near, far, at, msg):
    def block(first, second, rows):
        ix = {near: first, far: second}
        return buf.at[c, ix["x"], ix["z"], rows]

    low, high, whole = pl.ds(0, ROWS), pl.ds(ROWS, ROWS), pl.ds(0, 2 * ROWS)
    if msg == 0:
        return block(at[near], at[far], pl.ds(pl.multiple_of(at["h"] * ROWS, 16), ROWS))
    if msg in (1, 2):
        return block(at[near], at[far], whole)
    if msg == 3:
        return block(shifted(at, near, -1)[near], at[far], low)
    if msg == 4:
        return block(shifted(at, near, 1)[near], at[far], high)
    if msg in (5, 6):
        return block(pl.ds(0, 4), at[far], whole)
    if msg == 7:
        return block(pl.ds(0, 2), shifted(at, far, -1)[far], whole)
    return block(pl.ds(2, 2), shifted(at, far, 1)[far], whole)


def moves(near, far):
    return (("h", 1), (near, 1), (near, -1), (near, 1), (near, -1), (far, 1), (far, -1), (far, 1), (far, -1))


STAGES = ((0,), (1, 2), (3, 4), (5, 6), (7, 8))


def kernel(
    x_ref, og_ref, ib_ref, gb_ref, eg_ref, out_ref,
    ga, gb2, go, ib, gbt, tot, qot, ev, inv, q, ti, v, r, part, lpart,
    ib_sem, ev_sem, own_sem, a_send, a_recv, ga_send, ga_recv, gb_send, gb_recv, r_send, r_recv, l_send, l_recv,
):
    me = lax.axis_index("shard")
    layer = lax.axis_index("layer")
    at = where_am_i()
    halves = (
        (ga, ga_send, ga_recv, "x", "z"),
        (gb2, gb_send, gb_recv, "z", "x"),
    )

    def basis_copy(c):
        return pltpu.make_async_copy(ib_ref.at[c], ib.at[c], ib_sem.at[c])

    def eig_copy(c, slot):
        cols = pl.ds(pl.multiple_of(c * BLK, BLK), BLK)
        return pltpu.make_async_copy(eg_ref.at[:, cols], ev.at[slot], ev_sem.at[slot])

    for c in range(CHUNKS):
        basis_copy(c).start()
    eig_copy(0, 0).start()

    bar = pltpu.get_barrier_semaphore()

    def greet(i, _):
        pl.semaphore_signal(bar, inc=1, device_id=(layer, (me + i) % SHARDS), device_id_type=MESH)
        return 0

    lax.fori_loop(1, SHARDS, greet, 0)
    for i in range(1, LAYERS):
        pl.semaphore_signal(bar, inc=1, device_id=((layer + i) % LAYERS, me), device_id_type=MESH)
    pl.semaphore_wait(bar, SHARDS - 1 + LAYERS - 1)

    def rows_of(s):
        return pl.ds(pl.multiple_of(s * ROWS, 16), ROWS)

    def cols_of(s):
        return pl.ds(pl.multiple_of(s * BLK, BLK), BLK)

    def column_send(i):
        to = (me + i) % SHARDS
        return pltpu.make_async_remote_copy(
            src_ref=og_ref.at[:, cols_of(to)], dst_ref=go.at[rows_of(me)],
            send_sem=a_send.at[i], recv_sem=a_recv.at[i], device_id=(layer, to), device_id_type=MESH,
        )

    def column_recv(i):
        frm = (me + SHARDS - i) % SHARDS
        return pltpu.make_async_remote_copy(
            src_ref=og_ref.at[:, cols_of(me)], dst_ref=go.at[rows_of(frm)],
            send_sem=a_send.at[i], recv_sem=a_recv.at[i], device_id=(layer, frm), device_id_type=MESH,
        )

    own = pltpu.make_async_copy(og_ref.at[:, cols_of(me)], go.at[rows_of(me)], own_sem)
    own.start()

    def message(half, c, msg, receive):
        buf, send, recv, near, far = halves[half]
        axis, step = moves(near, far)[msg]
        sender = shifted(at, axis, -step) if receive else at
        piece = region(buf, c, near, far, sender, msg)
        return pltpu.make_async_remote_copy(
            src_ref=piece, dst_ref=piece, send_sem=send.at[c, msg], recv_sem=recv.at[c, msg],
            device_id=device_of(shifted(at, axis, step)), device_id_type=MESH,
        )

    def stage(half, number, c):
        def go_on():
            if number > 0:
                for msg in STAGES[number - 1]:
                    message(half, c, msg, True).wait_recv()
            if number < len(STAGES):
                for msg in STAGES[number]:
                    message(half, c, msg, False).start()

        return go_on

    def step_half(half, k):
        for number, lag in ((4, -3), (3, -2), (2, -1), (1, 0), (0, 2)):
            c = k + lag
            pl.when(jnp.logical_and(c >= 0, c < CHUNKS))(stage(half, number, c))

    def project(c, _):
        basis_copy(c).wait()
        mine = jnp.dot(x_ref[:, cols_of(c)], ib[c], preferred_element_type=F32).astype(BF)
        here = pl.ds(pl.multiple_of(at["h"] * ROWS, 16), ROWS)
        ga[c, at["x"], at["z"], here, :] = mine[:, :HALF]
        gb2[c, at["x"], at["z"], here, :] = mine[:, HALF:]

        @pl.when(c < 2)
        def _():
            for half in range(2):
                message(half, c, 0, False).start()

        return 0

    lax.fori_loop(0, 2, project, 0)

    def send_columns(i, _):
        column_send(i).start()
        return 0

    lax.fori_loop(1, SHARDS, send_columns, 0)
    lax.fori_loop(2, CHUNKS, project, 0)
    gbt[...] = gb_ref[...].T
    r[...] = jnp.zeros_like(r)

    def fill(k, _):
        step_half(0, k)
        step_half(1, k)
        return 0

    lax.fori_loop(0, LEAD, fill, 0)

    own.wait()

    def take_columns(i, _):
        column_recv(i).wait_recv()
        return 0

    lax.fori_loop(1, SHARDS, take_columns, 0)

    def turned(rows):
        return lax.dot_general(
            gbt[...], go[rows, :], (((1,), (1,)), ((), ())), preferred_element_type=F32
        ).astype(BF)

    qot[...] = turned(pl.ds(0, QTOK)).astype(F32)

    def turn_train(t, _):
        tot[t] = turned(pl.ds(pl.multiple_of(QTOK + t * ST, ST), ST))
        return 0

    lax.fori_loop(0, NT, turn_train, 0)

    def compute(k):
        c = k - LEAD
        slot = c % 2
        for half in range(2):
            for msg in STAGES[4]:
                message(half, c, msg, True).wait_recv()
        eig_copy(c, slot).wait()

        @pl.when(c + 1 < CHUNKS)
        def _():
            eig_copy(c + 1, 1 - slot).start()

        inv[...] = 1.0 / (ev[slot] + DAMPING)
        for half, buf in enumerate((ga, gb2)):
            cols = slice(half * HALF, half * HALF + HALF)
            q[0:384, cols] = buf[c, 0].reshape(384, HALF)
            q[384:480, cols] = buf[c, 1, 0]
            q[480:512, cols] = buf[c, 1, 1, 0:32]
            ti[0:64, cols] = buf[c, 1, 1, 32:96]
            ti[64:160, cols] = buf[c, 1, 2]
            ti[160:256, cols] = buf[c, 1, 3]
            ti[256:640, cols] = buf[c, 2].reshape(384, HALF)
            ti[640:1024, cols] = buf[c, 3].reshape(384, HALF)

        def group(g, _):
            @pl.when(g == 2)
            def _():
                step_half(1, k)

            for n in range(GROUP):
                t = g * GROUP + n
                grad = jnp.dot(tot[t], ti[pl.ds(pl.multiple_of(t * ST, ST), ST), :], preferred_element_type=F32)
                v[n * BLK : (n + 1) * BLK, :] = (grad * inv[...]).astype(BF)
            for o in range(0, QTOK, 256):
                z = lax.dot_general(
                    v[...], q[o : o + 256, :], (((1,), (1,)), ((), ())), preferred_element_type=F32
                )
                for n in range(GROUP):
                    t = g * GROUP + n
                    r[pl.ds(t, 1), o : o + 256] += jnp.sum(
                        z[n * BLK : (n + 1) * BLK] * qot[:, o : o + 256], axis=0, keepdims=True
                    )
            return 0

        lax.fori_loop(0, NT // GROUP, group, 0)

    def main(k, _):
        step_half(0, k)
        compute(k)
        return 0

    lax.fori_loop(LEAD, CHUNKS + LEAD, main, 0)

    token = lax.broadcasted_iota(jnp.int32, (QTOK, 128), 0) // SQ
    query = lax.broadcasted_iota(jnp.int32, (QTOK, 128), 1)
    marks = (token == query).astype(F32)
    norm_factor = 1.0 / math.sqrt(BLK * SHARDS * D * SQ * ST)
    part[me] = norm_factor * jnp.dot(r[...], marks, preferred_element_type=F32, precision=lax.Precision.HIGHEST)

    def part_copy(i, receive):
        to = (me + i) % SHARDS
        slot = (me + SHARDS - i) % SHARDS if receive else me
        return pltpu.make_async_remote_copy(
            src_ref=part.at[slot], dst_ref=part.at[slot], send_sem=r_send.at[i], recv_sem=r_recv.at[i],
            device_id=(layer, to), device_id_type=MESH,
        )

    def layer_copy(i, receive):
        to = (layer + i) % LAYERS
        slot = (layer + LAYERS - i) % LAYERS if receive else layer
        return pltpu.make_async_remote_copy(
            src_ref=lpart.at[slot], dst_ref=lpart.at[slot], send_sem=l_send.at[i], recv_sem=l_recv.at[i],
            device_id=(to, me), device_id_type=MESH,
        )

    def part_start(i, _):
        part_copy(i, False).start()
        return 0

    def part_take(i, _):
        part_copy(i, True).wait_recv()
        return 0

    lax.fori_loop(1, SHARDS, part_start, 0)
    lax.fori_loop(1, SHARDS, part_take, 0)
    lpart[layer] = jnp.sum(part[...], axis=0)
    for i in range(1, LAYERS):
        layer_copy(i, False).start()
    for i in range(1, LAYERS):
        layer_copy(i, True).wait_recv()
    out_ref[...] = lpart[...]

    def sent(i, _):
        column_send(i).wait_send()
        part_copy(i, False).wait_send()
        return 0

    lax.fori_loop(1, SHARDS, sent, 0)
    for i in range(1, LAYERS):
        layer_copy(i, False).wait_send()

    def chunk_sent(c, _):
        for half in range(2):
            for msg in range(9):
                message(half, c, msg, False).wait_send()
        return 0

    lax.fori_loop(0, CHUNKS, chunk_sent, 0)


def layer_parts(layer_inputs, output_grads, input_basis, grad_basis, eigenvalues):
    vmem = pl.BlockSpec(memory_space=pltpu.VMEM)
    hbm = pl.BlockSpec(memory_space=pl.ANY)
    dma = pltpu.SemaphoreType.DMA
    scratch = [
        pltpu.VMEM((CHUNKS, 4, 4, 2 * ROWS, HALF), BF),
        pltpu.VMEM((CHUNKS, 4, 4, 2 * ROWS, HALF), BF),
        pltpu.VMEM((SHARDS * ROWS, BLK), BF),
        pltpu.VMEM((CHUNKS, BLK, BLK), BF),
        pltpu.VMEM((BLK, BLK), BF),
        pltpu.VMEM((NT, BLK, ST), BF),
        pltpu.VMEM((BLK, QTOK), F32),
        pltpu.VMEM((2, BLK, BLK), F32),
        pltpu.VMEM((BLK, BLK), F32),
        pltpu.VMEM((QTOK, BLK), BF),
        pltpu.VMEM((NT * ST, BLK), BF),
        pltpu.VMEM((GROUP * BLK, BLK), BF),
        pltpu.VMEM((NT, QTOK), F32),
        pltpu.VMEM((SHARDS, NT, 128), F32),
        pltpu.VMEM((LAYERS, NT, 128), F32),
        dma((CHUNKS,)), dma((2,)), dma,
        dma((SHARDS,)), dma((SHARDS,)),
        dma((CHUNKS, 9)), dma((CHUNKS, 9)), dma((CHUNKS, 9)), dma((CHUNKS, 9)),
        dma((SHARDS,)), dma((SHARDS,)),
        dma((LAYERS,)), dma((LAYERS,)),
    ]
    return pl.pallas_call(
        kernel,
        out_shape=jax.ShapeDtypeStruct((LAYERS, NT, 128), F32),
        in_specs=[vmem, hbm, hbm, vmem, hbm],
        out_specs=vmem,
        scratch_shapes=scratch,
        compiler_params=pltpu.CompilerParams(
            collective_id=0, has_side_effects=True, vmem_limit_bytes=56 * 2**20
        ),
    )(layer_inputs, output_grads, input_basis, grad_basis, eigenvalues)


def per_device(
    layer_inputs, output_grads, input_basis, grad_basis, eigenvalues, layer_table, batch_ids
):
    parts = layer_parts(
        layer_inputs[0], output_grads[0], input_basis[0], grad_basis[0, 0], eigenvalues[0]
    )
    layer_scores = jnp.swapaxes(parts[:, :, :NQ], 1, 2)
    scores = jnp.sum(layer_scores, axis=0)
    batch_marks = (batch_ids[:, None] == jnp.arange(NB, dtype=jnp.int32)[None, :]).astype(F32)
    batch_scores = jnp.sum(scores[:, :, None] * batch_marks[None, :, :], axis=1)
    layer_marks = (layer_table[:, None] == jnp.arange(LAYERS, dtype=jnp.int32)[None, :]).astype(F32)
    layer_sums = jnp.sum(layer_scores, axis=2)
    layer_totals = jnp.sum(layer_marks[:, :, None] * layer_sums[:, None, :], axis=0)
    return (scores, batch_scores, layer_totals)


def solution(mesh):
    in_specs = (
        P("layer", "shard", None),
        P("layer", "shard", None),
        P("layer", None, None, None),
        P("layer", "shard", None, None),
        P("layer", "shard", None),
        P(),
        P(),
    )
    out_specs = (P(), P(), P())
    return jax.shard_map(
        per_device, mesh=mesh, in_specs=in_specs, out_specs=out_specs, check_vma=False
    )
```

```python
import functools
import math

import jax
import jax.numpy as jnp
from jax import lax
from jax.experimental import pallas as pl
from jax.experimental.pallas import tpu as pltpu
from jax.sharding import PartitionSpec as P

NQ = 16
SQ = 32
NT = 16
ST = 64
NB = 4
DAMPING = 0.1

D = 5120
BLK = 512
CHUNKS = D // BLK
HALF = BLK // 2
SHARDS = 32
LAYERS = 4
ROWS = 48
QTOK = NQ * SQ
GROUP = 4
LEAD = 4
TIMES = (0, 3, 6, 10, 13)
INVERSE_TIME = 4
COLUMNS_AT_ONCE = 3
MESSAGES = ((0, 1, 2), (3, 4), (5, 6))
MESH = pl.DeviceIdType.MESH
F32 = jnp.float32
BF = jnp.bfloat16


def kernel(
    x_ref, og_ref, ib_ref, gb_ref, eg_ref, out_ref,
    gath, mine, go, ib, ev, inv_out, inv_in, gb_in, gbt, tot, qot, inv, q, ti, v, r, px, pz, pp,
    ib_sem, ev_sem, own_sem, a_send, a_recv, b_send, b_recv, i_send, i_recv,
    p_send, p_recv, g_send, g_recv, s_send, s_recv, x_send, x_recv, z_send, z_recv, l_send, l_recv,
):
    shard, layer = lax.axis_index("shard"), lax.axis_index("layer")
    yl, core = layer // 2, layer % 2
    x, z, h = shard // 8, (shard // 2) % 4, shard % 2
    diag = core == h
    apart = core != h

    def device(yl, core, x, z, h):
        return (yl * 2 + core, (x * 4 + z) * 2 + h)

    def device_at(yl, core, place, h):
        return (yl * 2 + core, place * 2 + h)

    partner = device(yl, h, x, z, core)
    near, far = jnp.where(core == 0, x, z), jnp.where(core == 0, z, x)

    def beside(step_near, step_far):
        n, f = (near + step_near + 4) % 4, (far + step_far + 4) % 4
        return device(yl, core, jnp.where(core == 0, n, f), jnp.where(core == 0, f, n), h)

    def remote(src, dst, send, recv, to):
        return pltpu.make_async_remote_copy(
            src_ref=src, dst_ref=dst, send_sem=send, recv_sem=recv, device_id=to, device_id_type=MESH
        )

    def rows_of(s):
        return pl.ds(pl.multiple_of(s * ROWS, 16), ROWS)

    def cols_of(s):
        return pl.ds(pl.multiple_of(s * BLK, BLK), BLK)

    def basis_copy(c):
        return pltpu.make_async_copy(ib_ref.at[c], ib.at[c], ib_sem.at[c])

    def eig_copy(c):
        return pltpu.make_async_copy(eg_ref.at[:, cols_of(c)], ev.at[c], ev_sem.at[c])

    for c in range(CHUNKS):
        basis_copy(c).start()
    for c in range(CHUNKS):
        eig_copy(c).start()

    bar = pltpu.get_barrier_semaphore()

    def signal(to):
        pl.semaphore_signal(bar, inc=1, device_id=to, device_id_type=MESH)

    def greet(s, _):
        pl.when(jnp.logical_or(apart, s != shard))(lambda: signal((yl * 2 + h, s)))
        return 0

    lax.fori_loop(0, SHARDS, greet, 0)
    for i in range(1, 4):
        signal(beside(i, 0))
        signal(beside(0, i))
    plane = (yl * 2 + h) * 2 + core

    def across(i):
        p = (plane + i) % 8
        return device(p // 4, p % 2, x, z, (p // 2) % 2)

    for i in range(1, 8):
        signal(across(i))

    def project(c, _):
        basis_copy(c).wait()
        got = jnp.dot(x_ref[:, cols_of(c)], ib[c], preferred_element_type=F32).astype(BF)
        for half in range(2):
            mine[half, c] = got[:, half * HALF : (half + 1) * HALF]
        return 0

    lax.fori_loop(0, CHUNKS, project, 0)

    def column_send(to):
        return remote(
            og_ref.at[:, cols_of(to)], go.at[rows_of(shard)], a_send.at[to], a_recv.at[shard],
            device_at(yl, to % 2, to // 2, core),
        )

    def column_recv(s):
        return remote(
            og_ref.at[:, cols_of(s)], go.at[rows_of(s)], a_send.at[s], a_recv.at[s], (yl * 2 + h, s)
        )

    own = pltpu.make_async_copy(og_ref.at[:, cols_of(shard)], go.at[rows_of(shard)], own_sem)

    def other(s):
        return jnp.logical_or(apart, s != shard)

    def part_at(half, c, s):
        n, f = (x, z) if half == 0 else (z, x)
        return gath.at[half, c, n, f, pl.ds(pl.multiple_of(s * ROWS, 16), ROWS)]

    def part_send(half, c):
        return remote(
            mine.at[half, c], part_at(half, c, h), p_send.at[c, half], p_recv.at[c, h],
            device(yl, half, x, z, core),
        )

    def stays(half):
        return jnp.logical_and(diag, core == half)

    def part_recv(c, s):
        place = gath.at[core, c, near, far, pl.ds(s * ROWS, ROWS)]
        return remote(mine.at[0, c], place, p_send.at[c, 0], p_recv.at[c, s], device(yl, h, x, z, s))

    def message(c, msg, receive):
        if msg < 3:
            step = msg + 1
            back = 4 - step if receive else 0
            piece, to = gath.at[core, c, (near + back) % 4, far], beside(step, 0)
        else:
            step = 1 if msg % 2 else -1
            back = 4 - step if receive else 4
            blocks = pl.ds(0, 4) if msg < 5 else pl.ds(0, 2) if msg == 5 else pl.ds(2, 2)
            place = (far + back) % 4 if msg < 5 else (far + back - step) % 4
            piece, to = gath.at[core, c, blocks, place], beside(0, step)
        return remote(piece, piece, g_send.at[c, msg], g_recv.at[c, msg], to)

    def sibling(c, receive):
        half = 1 - core if receive else core
        return remote(
            gath.at[half, c], gath.at[half, c], s_send.at[c], s_recv.at[c], device(yl, 1 - core, x, z, h)
        )

    def inverse_copy(c):
        return remote(inv_out.at[c], inv_in.at[c], i_send.at[c], i_recv.at[c], partner)

    def inverse(c):
        eig_copy(c).wait()
        value = (1.0 / (ev[c] + DAMPING)).astype(BF)

        @pl.when(diag)
        def _():
            inv_in[c] = value

        @pl.when(apart)
        def _():
            inv_out[c] = value
            inverse_copy(c).start()

    def stage(number, c):
        if number == 0:
            for half in range(2):

                @pl.when(stays(half))
                def _():
                    n, f = (x, z) if half == 0 else (z, x)
                    gath[half, c, n, f, rows_of(h), :] = mine[half, c]

                pl.when(jnp.logical_not(stays(half)))(lambda: part_send(half, c).start())
            return
        if number == 1:
            for s in range(2):
                pl.when(jnp.logical_or(apart, h != s))(lambda: part_recv(c, s).wait_recv())
        else:
            for msg in MESSAGES[number - 2]:
                message(c, msg, True).wait_recv()
        if number < 4:
            for msg in MESSAGES[number - 1]:
                message(c, msg, False).start()
        else:
            sibling(c, False).start()

    def within(c, go_on):
        pl.when(jnp.logical_and(c >= 0, c < CHUNKS))(go_on)

    def quarter(k, g):
        for number in (4, 3, 2, 1, 0):
            when = TIMES[number]
            if when % 4 == g:
                within(k - when // 4, functools.partial(stage, number, k - when // 4))
        if INVERSE_TIME % 4 == g:
            within(k - INVERSE_TIME // 4, functools.partial(inverse, k - INVERSE_TIME // 4))

    pl.semaphore_wait(bar, 13 + SHARDS - diag.astype(jnp.int32))

    def basis_out():
        return remote(gb_ref, gb_in, b_send, b_recv, partner)

    pl.when(apart)(lambda: basis_out().start())

    def send_columns(i, _):
        to = (shard + i) % SHARDS
        pl.when(other(to))(lambda: column_send(to).start())
        return 0

    pl.when(diag)(own.start)
    start = min(TIMES + (INVERSE_TIME,)) // 4

    def fill(k, _):
        for g in range(4):
            quarter(k, g)
            first = (4 * (k - start) + g) * COLUMNS_AT_ONCE
            lax.fori_loop(jnp.minimum(first, SHARDS), jnp.minimum(first + COLUMNS_AT_ONCE, SHARDS), send_columns, 0)
        return 0

    lax.fori_loop(start, LEAD, fill, 0)

    @pl.when(diag)
    def _():
        gbt[...] = gb_ref[...].T

    @pl.when(apart)
    def _():
        basis_out().wait_recv()
        gbt[...] = gb_in[...].T

    r[...] = jnp.zeros_like(r)
    pl.when(diag)(own.wait)

    def take_columns(s, _):
        pl.when(other(s))(lambda: column_recv(s).wait_recv())
        return 0

    lax.fori_loop(0, SHARDS, take_columns, 0)

    def turned(rows):
        return lax.dot_general(
            gbt[...], go[rows, :], (((1,), (1,)), ((), ())), preferred_element_type=F32
        ).astype(BF)

    qot[...] = turned(pl.ds(0, QTOK)).astype(F32)

    def compute(k):
        c = k - LEAD
        sibling(c, True).wait_recv()
        pl.when(apart)(lambda: inverse_copy(c).wait_recv())
        inv[...] = inv_in[c].astype(F32)
        for half in range(2):
            cols = slice(half * HALF, half * HALF + HALF)
            for b in range(16):
                n, f = (b // 4, b % 4) if half == 0 else (b % 4, b // 4)
                first, last = 2 * ROWS * b, 2 * ROWS * (b + 1)
                cut = min(max(QTOK - first, 0), 2 * ROWS)
                if cut > 0:
                    q[first : first + cut, cols] = gath[half, c, n, f, :cut]
                if cut < 2 * ROWS:
                    ti[first + cut - QTOK : last - QTOK, cols] = gath[half, c, n, f, cut:]

        def group(g, _):
            for part_of in range(4):
                pl.when(g == part_of)(functools.partial(quarter, k, part_of))

            @pl.when(c == 0)
            def _():
                wide = GROUP * ST
                got = turned(pl.ds(pl.multiple_of(QTOK + g * wide, wide), wide))
                for n in range(GROUP):
                    tot[g * GROUP + n] = got[:, n * ST : (n + 1) * ST]

            for n in range(GROUP):
                t = g * GROUP + n
                grad = jnp.dot(tot[t], ti[pl.ds(pl.multiple_of(t * ST, ST), ST), :], preferred_element_type=F32)
                v[n * BLK : (n + 1) * BLK, :] = (grad * inv[...]).astype(BF)
            for o in range(0, QTOK, 256):
                part = lax.dot_general(
                    v[...], q[o : o + 256, :], (((1,), (1,)), ((), ())), preferred_element_type=F32
                )
                for n in range(GROUP):
                    t = g * GROUP + n
                    r[pl.ds(t, 1), o : o + 256] += jnp.sum(
                        part[n * BLK : (n + 1) * BLK] * qot[:, o : o + 256], axis=0, keepdims=True
                    )
            return 0

        lax.fori_loop(0, NT // GROUP, group, 0)

    def main(k, _):
        compute(k)
        return 0

    lax.fori_loop(LEAD, CHUNKS + LEAD, main, 0)

    token = lax.broadcasted_iota(jnp.int32, (QTOK, 128), 0) // SQ
    query = lax.broadcasted_iota(jnp.int32, (QTOK, 128), 1)
    marks = (token == query).astype(F32)
    norm_factor = 1.0 / math.sqrt(BLK * SHARDS * D * SQ * ST)

    def near_copy(i, receive):
        slot = (near + 4 - i) % 4 if receive else near
        return remote(px.at[slot], px.at[slot], x_send.at[i], x_recv.at[i], beside(i, 0))

    def far_copy(i, receive):
        slot = (far + 4 - i) % 4 if receive else far
        return remote(pz.at[slot], pz.at[slot], z_send.at[i], z_recv.at[i], beside(0, i))

    def plane_copy(i, receive):
        slot = (plane + 8 - i) % 8 if receive else plane
        return remote(pp.at[slot], pp.at[slot], l_send.at[i], l_recv.at[i], across(i))

    px[near] = norm_factor * jnp.dot(r[...], marks, preferred_element_type=F32, precision=lax.Precision.HIGHEST)
    for i in range(1, 4):
        near_copy(i, False).start()

    def columns_sent(to, _):
        pl.when(other(to))(lambda: column_send(to).wait_send())
        return 0

    lax.fori_loop(0, SHARDS, columns_sent, 0)

    def chunk_sent(c, _):
        for half in range(2):
            pl.when(jnp.logical_not(stays(half)))(lambda: part_send(half, c).wait_send())
        for msg in range(7):
            message(c, msg, False).wait_send()
        sibling(c, False).wait_send()
        pl.when(apart)(lambda: inverse_copy(c).wait_send())
        return 0

    lax.fori_loop(0, CHUNKS, chunk_sent, 0)
    pl.when(apart)(lambda: basis_out().wait_send())

    for i in range(1, 4):
        near_copy(i, True).wait_recv()
    pz[far] = jnp.sum(px[...], axis=0)
    for i in range(1, 4):
        far_copy(i, False).start()
    for i in range(1, 4):
        far_copy(i, True).wait_recv()
    pp[plane] = jnp.sum(pz[...], axis=0)
    for i in range(1, 8):
        plane_copy(i, False).start()
    for i in range(1, 4):
        near_copy(i, False).wait_send()
        far_copy(i, False).wait_send()
    for i in range(1, 8):
        plane_copy(i, True).wait_recv()
    out_ref[...] = pp[...]
    for i in range(1, 8):
        plane_copy(i, False).wait_send()


def layer_parts(layer_inputs, output_grads, input_basis, grad_basis, eigenvalues):
    vmem = pl.BlockSpec(memory_space=pltpu.VMEM)
    hbm = pl.BlockSpec(memory_space=pl.ANY)
    dma = pltpu.SemaphoreType.DMA
    scratch = [
        pltpu.VMEM((2, CHUNKS, 4, 4, 2 * ROWS, HALF), BF),
        pltpu.VMEM((2, CHUNKS, ROWS, HALF), BF),
        pltpu.VMEM((SHARDS * ROWS, BLK), BF),
        pltpu.VMEM((CHUNKS, BLK, BLK), BF),
        pltpu.VMEM((CHUNKS, BLK, BLK), F32),
        pltpu.VMEM((CHUNKS, BLK, BLK), BF),
        pltpu.VMEM((CHUNKS, BLK, BLK), BF),
        pltpu.VMEM((BLK, BLK), BF),
        pltpu.VMEM((BLK, BLK), BF),
        pltpu.VMEM((NT, BLK, ST), BF),
        pltpu.VMEM((BLK, QTOK), F32),
        pltpu.VMEM((BLK, BLK), F32),
        pltpu.VMEM((QTOK, BLK), BF),
        pltpu.VMEM((NT * ST, BLK), BF),
        pltpu.VMEM((GROUP * BLK, BLK), BF),
        pltpu.VMEM((NT, QTOK), F32),
        pltpu.VMEM((4, NT, 128), F32),
        pltpu.VMEM((4, NT, 128), F32),
        pltpu.VMEM((8, NT, 128), F32),
        dma((CHUNKS,)), dma((CHUNKS,)), dma,
        dma((SHARDS,)), dma((SHARDS,)), dma, dma, dma((CHUNKS,)), dma((CHUNKS,)),
        dma((CHUNKS, 2)), dma((CHUNKS, 2)), dma((CHUNKS, 7)), dma((CHUNKS, 7)), dma((CHUNKS,)), dma((CHUNKS,)),
        dma((4,)), dma((4,)), dma((4,)), dma((4,)), dma((8,)), dma((8,)),
    ]
    return pl.pallas_call(
        kernel,
        out_shape=jax.ShapeDtypeStruct((8, NT, 128), F32),
        in_specs=[vmem, hbm, hbm, vmem, hbm],
        out_specs=vmem,
        scratch_shapes=scratch,
        compiler_params=pltpu.CompilerParams(
            collective_id=0, has_side_effects=True, vmem_limit_bytes=60 * 2**20
        ),
    )(layer_inputs, output_grads, input_basis, grad_basis, eigenvalues)


def per_device(
    layer_inputs, output_grads, input_basis, grad_basis, eigenvalues, layer_table, batch_ids
):
    parts = layer_parts(
        layer_inputs[0], output_grads[0], input_basis[0], grad_basis[0, 0], eigenvalues[0]
    )
    per_layer = jnp.sum(parts.reshape(LAYERS, 2, NT, 128), axis=1)
    layer_scores = jnp.swapaxes(per_layer[:, :, :NQ], 1, 2)
    scores = jnp.sum(layer_scores, axis=0)
    batch_marks = (batch_ids[:, None] == jnp.arange(NB, dtype=jnp.int32)[None, :]).astype(F32)
    batch_scores = jnp.sum(scores[:, :, None] * batch_marks[None, :, :], axis=1)
    layer_marks = (layer_table[:, None] == jnp.arange(LAYERS, dtype=jnp.int32)[None, :]).astype(F32)
    layer_sums = jnp.sum(layer_scores, axis=2)
    layer_totals = jnp.sum(layer_marks[:, :, None] * layer_sums[:, None, :], axis=0)
    return (scores, batch_scores, layer_totals)


def solution(mesh):
    in_specs = (
        P("layer", "shard", None),
        P("layer", "shard", None),
        P("layer", None, None, None),
        P("layer", "shard", None, None),
        P("layer", "shard", None),
        P(),
        P(),
    )
    out_specs = (P(), P(), P())
    return jax.shard_map(
        per_device, mesh=mesh, in_specs=in_specs, out_specs=out_specs, check_vma=False
    )
```

```python
import functools
import math

import jax
import jax.numpy as jnp
from jax import lax
from jax.experimental import pallas as pl
from jax.experimental.pallas import tpu as pltpu
from jax.sharding import PartitionSpec as P

NQ = 16
SQ = 32
NT = 16
ST = 64
NB = 4
DAMPING = 0.1

D = 5120
BLK = 512
CHUNKS = D // BLK
HALF = BLK // 2
SHARDS = 32
LAYERS = 4
ROWS = 48
QTOK = NQ * SQ
GROUP = 4
LEAD = 4
TIMES = (0, 3, 6, 10, 13)
INVERSE_TIME = 4
COLUMNS_AT_ONCE = 3
MESSAGES = ((0, 1, 2), (3, 4), (5, 6))
MESH = pl.DeviceIdType.MESH
F32 = jnp.float32
BF = jnp.bfloat16


def kernel(
    x_ref, og_ref, ib_ref, gb_ref, eg_ref, out_ref,
    gath, mine, go, ib, ev, inv_out, inv_in, gb_in, gbt, tot, qot, inv, q, ti, v, r, px, pz, pp,
    ib_sem, ev_sem, own_sem, a_send, a_recv, b_send, b_recv, i_send, i_recv,
    p_send, p_recv, g_send, g_recv, s_send, s_recv, x_send, x_recv, z_send, z_recv, l_send, l_recv,
):
    shard, layer = lax.axis_index("shard"), lax.axis_index("layer")
    yl, core = layer // 2, layer % 2
    x, z, h = shard // 8, (shard // 2) % 4, shard % 2
    diag = core == h
    apart = core != h

    def device(yl, core, x, z, h):
        return (yl * 2 + core, (x * 4 + z) * 2 + h)

    def device_at(yl, core, place, h):
        return (yl * 2 + core, place * 2 + h)

    partner = device(yl, h, x, z, core)
    near, far = jnp.where(core == 0, x, z), jnp.where(core == 0, z, x)

    def beside(step_near, step_far):
        n, f = (near + step_near + 4) % 4, (far + step_far + 4) % 4
        return device(yl, core, jnp.where(core == 0, n, f), jnp.where(core == 0, f, n), h)

    def remote(src, dst, send, recv, to):
        return pltpu.make_async_remote_copy(
            src_ref=src, dst_ref=dst, send_sem=send, recv_sem=recv, device_id=to, device_id_type=MESH
        )

    def rows_of(s):
        return pl.ds(pl.multiple_of(s * ROWS, 16), ROWS)

    def cols_of(s):
        return pl.ds(pl.multiple_of(s * BLK, BLK), BLK)

    def basis_copy(c):
        return pltpu.make_async_copy(ib_ref.at[c], ib.at[c], ib_sem.at[c])

    def eig_copy(c):
        return pltpu.make_async_copy(eg_ref.at[:, cols_of(c)], ev.at[c], ev_sem.at[c])

    for c in range(CHUNKS):
        basis_copy(c).start()
    for c in range(CHUNKS):
        eig_copy(c).start()

    bar = pltpu.get_barrier_semaphore()

    def signal(to):
        pl.semaphore_signal(bar, inc=1, device_id=to, device_id_type=MESH)

    def greet(s, _):
        pl.when(jnp.logical_or(apart, s != shard))(lambda: signal((yl * 2 + h, s)))
        return 0

    lax.fori_loop(0, SHARDS, greet, 0)
    for i in range(1, 4):
        signal(beside(i, 0))
        signal(beside(0, i))
    plane = (yl * 2 + h) * 2 + core

    def across(i):
        p = (plane + i) % 8
        return device(p // 4, p % 2, x, z, (p // 2) % 2)

    for i in range(1, 8):
        signal(across(i))

    def project(c, _):
        basis_copy(c).wait()
        got = jnp.dot(x_ref[:, cols_of(c)], ib[c], preferred_element_type=F32).astype(BF)
        for half in range(2):
            mine[half, c] = got[:, half * HALF : (half + 1) * HALF]
        return 0

    lax.fori_loop(0, CHUNKS, project, 0)

    def column_send(to):
        return remote(
            og_ref.at[:, cols_of(to)], go.at[rows_of(shard)], a_send.at[to], a_recv.at[shard],
            device_at(yl, to % 2, to // 2, core),
        )

    def column_recv(s):
        return remote(
            og_ref.at[:, cols_of(s)], go.at[rows_of(s)], a_send.at[s], a_recv.at[s], (yl * 2 + h, s)
        )

    own = pltpu.make_async_copy(og_ref.at[:, cols_of(shard)], go.at[rows_of(shard)], own_sem)

    def other(s):
        return jnp.logical_or(apart, s != shard)

    def part_at(half, c, s):
        n, f = (x, z) if half == 0 else (z, x)
        return gath.at[half, c, n, f, pl.ds(pl.multiple_of(s * ROWS, 16), ROWS)]

    def part_send(half, c):
        return remote(
            mine.at[half, c], part_at(half, c, h), p_send.at[c, half], p_recv.at[c, h],
            device(yl, half, x, z, core),
        )

    def stays(half):
        return jnp.logical_and(diag, core == half)

    def part_recv(c, s):
        place = gath.at[core, c, near, far, pl.ds(s * ROWS, ROWS)]
        return remote(mine.at[0, c], place, p_send.at[c, 0], p_recv.at[c, s], device(yl, h, x, z, s))

    def message(c, msg, receive):
        if msg < 3:
            step = msg + 1
            back = 4 - step if receive else 0
            piece, to = gath.at[core, c, (near + back) % 4, far], beside(step, 0)
        else:
            step = 1 if msg % 2 else -1
            back = 4 - step if receive else 4
            blocks = pl.ds(0, 4) if msg < 5 else pl.ds(0, 2) if msg == 5 else pl.ds(2, 2)
            place = (far + back) % 4 if msg < 5 else (far + back - step) % 4
            piece, to = gath.at[core, c, blocks, place], beside(0, step)
        return remote(piece, piece, g_send.at[c, msg], g_recv.at[c, msg], to)

    def sibling(c, receive):
        half = 1 - core if receive else core
        return remote(
            gath.at[half, c], gath.at[half, c], s_send.at[c], s_recv.at[c], device(yl, 1 - core, x, z, h)
        )

    def inverse_copy(c):
        return remote(inv_out.at[c], inv_in.at[c], i_send.at[c], i_recv.at[c], partner)

    def inverse(c):
        eig_copy(c).wait()
        value = (1.0 / (ev[c] + DAMPING)).astype(BF)

        @pl.when(diag)
        def _():
            inv_in[c] = value

        @pl.when(apart)
        def _():
            inv_out[c] = value
            inverse_copy(c).start()

    def stage(number, c):
        if number == 0:
            for half in range(2):

                @pl.when(stays(half))
                def _():
                    n, f = (x, z) if half == 0 else (z, x)
                    gath[half, c, n, f, rows_of(h), :] = mine[half, c]

                pl.when(jnp.logical_not(stays(half)))(lambda: part_send(half, c).start())
            return
        if number == 1:
            for s in range(2):
                pl.when(jnp.logical_or(apart, h != s))(lambda: part_recv(c, s).wait_recv())
        else:
            for msg in MESSAGES[number - 2]:
                message(c, msg, True).wait_recv()
        if number < 4:
            for msg in MESSAGES[number - 1]:
                message(c, msg, False).start()
        else:
            sibling(c, False).start()

    def within(c, go_on):
        pl.when(jnp.logical_and(c >= 0, c < CHUNKS))(go_on)

    def quarter(k, g):
        for number in (4, 3, 2, 1, 0):
            when = TIMES[number]
            if when % 4 == g:
                within(k - when // 4, functools.partial(stage, number, k - when // 4))
        if INVERSE_TIME % 4 == g:
            within(k - INVERSE_TIME // 4, functools.partial(inverse, k - INVERSE_TIME // 4))

    pl.semaphore_wait(bar, 13 + SHARDS - diag.astype(jnp.int32))

    def basis_out():
        return remote(gb_ref, gb_in, b_send, b_recv, partner)

    pl.when(apart)(lambda: basis_out().start())

    def send_columns(i, _):
        to = (shard + i) % SHARDS
        pl.when(other(to))(lambda: column_send(to).start())
        return 0

    pl.when(diag)(own.start)
    start = min(TIMES + (INVERSE_TIME,)) // 4

    hold = jnp.where(shard >= 22, 4, jnp.where(shard >= 16, 2, 0))

    def fill(k, _):
        for g in range(4):
            quarter(k, g)
            first = jnp.maximum(4 * (k - start) + g - hold, 0) * COLUMNS_AT_ONCE
            first = jnp.where(4 * (k - start) + g < hold, SHARDS, first)
            lax.fori_loop(jnp.minimum(first, SHARDS), jnp.minimum(first + COLUMNS_AT_ONCE, SHARDS), send_columns, 0)
        return 0

    lax.fori_loop(start, LEAD, fill, 0)

    @pl.when(diag)
    def _():
        gbt[...] = gb_ref[...].T

    @pl.when(apart)
    def _():
        basis_out().wait_recv()
        gbt[...] = gb_in[...].T

    r[...] = jnp.zeros_like(r)
    pl.when(diag)(own.wait)

    def take_columns(s, _):
        pl.when(other(s))(lambda: column_recv(s).wait_recv())
        return 0

    lax.fori_loop(0, -(-QTOK // ROWS), take_columns, 0)

    def turned(rows):
        return lax.dot_general(
            gbt[...], go[rows, :], (((1,), (1,)), ((), ())), preferred_element_type=F32
        ).astype(BF)

    qot[...] = turned(pl.ds(0, QTOK)).astype(F32)

    def compute(k):
        c = k - LEAD
        sibling(c, True).wait_recv()
        pl.when(apart)(lambda: inverse_copy(c).wait_recv())
        inv[...] = inv_in[c].astype(F32)
        for half in range(2):
            cols = slice(half * HALF, half * HALF + HALF)
            for b in range(16):
                n, f = (b // 4, b % 4) if half == 0 else (b % 4, b // 4)
                first, last = 2 * ROWS * b, 2 * ROWS * (b + 1)
                cut = min(max(QTOK - first, 0), 2 * ROWS)
                if cut > 0:
                    q[first : first + cut, cols] = gath[half, c, n, f, :cut]
                if cut < 2 * ROWS:
                    ti[first + cut - QTOK : last - QTOK, cols] = gath[half, c, n, f, cut:]

        def group(g, _):
            for part_of in range(4):
                pl.when(g == part_of)(functools.partial(quarter, k, part_of))

            @pl.when(c == 0)
            def _():
                wide = GROUP * ST
                need = QTOK - 1 + g * wide
                lax.fori_loop(need // ROWS + 1, (need + wide) // ROWS + 1, take_columns, 0)
                got = turned(pl.ds(pl.multiple_of(QTOK + g * wide, wide), wide))
                for n in range(GROUP):
                    tot[g * GROUP + n] = got[:, n * ST : (n + 1) * ST]

            for n in range(GROUP):
                t = g * GROUP + n
                grad = jnp.dot(tot[t], ti[pl.ds(pl.multiple_of(t * ST, ST), ST), :], preferred_element_type=F32)
                v[n * BLK : (n + 1) * BLK, :] = (grad * inv[...]).astype(BF)
            for o in range(0, QTOK, 256):
                part = lax.dot_general(
                    v[...], q[o : o + 256, :], (((1,), (1,)), ((), ())), preferred_element_type=F32
                )
                for n in range(GROUP):
                    t = g * GROUP + n
                    r[pl.ds(t, 1), o : o + 256] += jnp.sum(
                        part[n * BLK : (n + 1) * BLK] * qot[:, o : o + 256], axis=0, keepdims=True
                    )
            return 0

        lax.fori_loop(0, NT // GROUP, group, 0)

    def main(k, _):
        compute(k)
        return 0

    lax.fori_loop(LEAD, CHUNKS + LEAD, main, 0)

    token = lax.broadcasted_iota(jnp.int32, (QTOK, 128), 0) // SQ
    query = lax.broadcasted_iota(jnp.int32, (QTOK, 128), 1)
    marks = (token == query).astype(F32)
    norm_factor = 1.0 / math.sqrt(BLK * SHARDS * D * SQ * ST)

    def near_copy(i, receive):
        slot = (near + 4 - i) % 4 if receive else near
        return remote(px.at[slot], px.at[slot], x_send.at[i], x_recv.at[i], beside(i, 0))

    def far_copy(i, receive):
        slot = (far + 4 - i) % 4 if receive else far
        return remote(pz.at[slot], pz.at[slot], z_send.at[i], z_recv.at[i], beside(0, i))

    def plane_copy(i, receive):
        slot = (plane + 8 - i) % 8 if receive else plane
        return remote(pp.at[slot], pp.at[slot], l_send.at[i], l_recv.at[i], across(i))

    px[near] = norm_factor * jnp.dot(r[...], marks, preferred_element_type=F32, precision=lax.Precision.HIGHEST)
    for i in range(1, 4):
        near_copy(i, False).start()

    def columns_sent(to, _):
        pl.when(other(to))(lambda: column_send(to).wait_send())
        return 0

    lax.fori_loop(0, SHARDS, columns_sent, 0)

    def chunk_sent(c, _):
        for half in range(2):
            pl.when(jnp.logical_not(stays(half)))(lambda: part_send(half, c).wait_send())
        for msg in range(7):
            message(c, msg, False).wait_send()
        sibling(c, False).wait_send()
        pl.when(apart)(lambda: inverse_copy(c).wait_send())
        return 0

    lax.fori_loop(0, CHUNKS, chunk_sent, 0)
    pl.when(apart)(lambda: basis_out().wait_send())

    for i in range(1, 4):
        near_copy(i, True).wait_recv()
    pz[far] = jnp.sum(px[...], axis=0)
    for i in range(1, 4):
        far_copy(i, False).start()
    for i in range(1, 4):
        far_copy(i, True).wait_recv()
    pp[plane] = jnp.sum(pz[...], axis=0)
    for i in range(1, 8):
        plane_copy(i, False).start()
    for i in range(1, 4):
        near_copy(i, False).wait_send()
        far_copy(i, False).wait_send()
    for i in range(1, 8):
        plane_copy(i, True).wait_recv()
    out_ref[...] = pp[...]
    for i in range(1, 8):
        plane_copy(i, False).wait_send()


def layer_parts(layer_inputs, output_grads, input_basis, grad_basis, eigenvalues):
    vmem = pl.BlockSpec(memory_space=pltpu.VMEM)
    hbm = pl.BlockSpec(memory_space=pl.ANY)
    dma = pltpu.SemaphoreType.DMA
    scratch = [
        pltpu.VMEM((2, CHUNKS, 4, 4, 2 * ROWS, HALF), BF),
        pltpu.VMEM((2, CHUNKS, ROWS, HALF), BF),
        pltpu.VMEM((SHARDS * ROWS, BLK), BF),
        pltpu.VMEM((CHUNKS, BLK, BLK), BF),
        pltpu.VMEM((CHUNKS, BLK, BLK), F32),
        pltpu.VMEM((CHUNKS, BLK, BLK), BF),
        pltpu.VMEM((CHUNKS, BLK, BLK), BF),
        pltpu.VMEM((BLK, BLK), BF),
        pltpu.VMEM((BLK, BLK), BF),
        pltpu.VMEM((NT, BLK, ST), BF),
        pltpu.VMEM((BLK, QTOK), F32),
        pltpu.VMEM((BLK, BLK), F32),
        pltpu.VMEM((QTOK, BLK), BF),
        pltpu.VMEM((NT * ST, BLK), BF),
        pltpu.VMEM((GROUP * BLK, BLK), BF),
        pltpu.VMEM((NT, QTOK), F32),
        pltpu.VMEM((4, NT, 128), F32),
        pltpu.VMEM((4, NT, 128), F32),
        pltpu.VMEM((8, NT, 128), F32),
        dma((CHUNKS,)), dma((CHUNKS,)), dma,
        dma((SHARDS,)), dma((SHARDS,)), dma, dma, dma((CHUNKS,)), dma((CHUNKS,)),
        dma((CHUNKS, 2)), dma((CHUNKS, 2)), dma((CHUNKS, 7)), dma((CHUNKS, 7)), dma((CHUNKS,)), dma((CHUNKS,)),
        dma((4,)), dma((4,)), dma((4,)), dma((4,)), dma((8,)), dma((8,)),
    ]
    return pl.pallas_call(
        kernel,
        out_shape=jax.ShapeDtypeStruct((8, NT, 128), F32),
        in_specs=[vmem, hbm, hbm, vmem, hbm],
        out_specs=vmem,
        scratch_shapes=scratch,
        compiler_params=pltpu.CompilerParams(
            collective_id=0, has_side_effects=True, vmem_limit_bytes=60 * 2**20
        ),
    )(layer_inputs, output_grads, input_basis, grad_basis, eigenvalues)


def per_device(
    layer_inputs, output_grads, input_basis, grad_basis, eigenvalues, layer_table, batch_ids
):
    parts = layer_parts(
        layer_inputs[0], output_grads[0], input_basis[0], grad_basis[0, 0], eigenvalues[0]
    )
    per_layer = jnp.sum(parts.reshape(LAYERS, 2, NT, 128), axis=1)
    layer_scores = jnp.swapaxes(per_layer[:, :, :NQ], 1, 2)
    scores = jnp.sum(layer_scores, axis=0)
    batch_marks = (batch_ids[:, None] == jnp.arange(NB, dtype=jnp.int32)[None, :]).astype(F32)
    batch_scores = jnp.sum(scores[:, :, None] * batch_marks[None, :, :], axis=1)
    layer_marks = (layer_table[:, None] == jnp.arange(LAYERS, dtype=jnp.int32)[None, :]).astype(F32)
    layer_sums = jnp.sum(layer_scores, axis=2)
    layer_totals = jnp.sum(layer_marks[:, :, None] * layer_sums[:, None, :], axis=0)
    return (scores, batch_scores, layer_totals)


def solution(mesh):
    in_specs = (
        P("layer", "shard", None),
        P("layer", "shard", None),
        P("layer", None, None, None),
        P("layer", "shard", None, None),
        P("layer", "shard", None),
        P(),
        P(),
    )
    out_specs = (P(), P(), P())
    return jax.shard_map(
        per_device, mesh=mesh, in_specs=in_specs, out_specs=out_specs, check_vma=False
    )
```
